32 devices in a mesh: ctx: 4 (over z), head: 8 (over y, x, core).
Axes of the slice: x: 2, y: 2, z: 4, core: 2. Of those that a mesh axis runs over, the one named last changes fastest.
Arguments:
- queries: bfloat16 [12288, 4096], P('ctx', 'head'), may hold values from -64 to 64
- key_vectors: bfloat16 [12288, 4096], P('ctx', 'head'), may hold values from -5 to 5
- value_vectors: bfloat16 [12288, 4096], P('ctx', 'head'), may hold values from -6 to 6
- step_sizes: float32 [8, 12288], P('head', 'ctx'), may hold values from 0.0003 to 0.003
- w_in: bfloat16 [8, 512, 512], P('head'), may hold values from -0.25 to 0.25
- w_up: bfloat16 [8, 512, 512], P('head'), may hold values from -0.25 to 0.25
- w_out: bfloat16 [8, 512, 512], P('head'), may hold values from -0.125 to 0.125
- out_gate: bfloat16 [12288, 4096], P('ctx', 'head'), may hold values from -6 to 6
- norm_gain: float32 [4096], replicated, may hold values from 0.5 to 1.5
Outputs:
- layer_out: bfloat16 [12288, 4096], P(('ctx', 'head'))
The draws below stay inside these ranges and needn't reach their ends.
All inputs are finite; a program needn't handle non-finite values.
Results may differ from the reference program's by a relative error of at most 0.025.
Values may be sent and summed in bfloat16 or wider, within the bound.
A program may use at most 128 MiB of HBM per device.

```python
import math
import jax
import jax.numpy as jnp
from jax import lax

HD = 512
FH = 512
WINDOW = 1024
TOK_DEV = 3072
HEADS = 8
D = 4096
TOKENS = 12288
N_CTX = 4


def drawn_field(key, salt, limit):
    return jnp.clip(jax.random.normal(jax.random.fold_in(key, salt), (TOKENS, D), jnp.float32), -limit, limit)


def draw_queries(key, part):
    return drawn_field(key, 12, 4.0).astype(jnp.bfloat16)


def draw_key_vectors(key, part):
    return drawn_field(key, 11, 4.0).astype(jnp.bfloat16)


def shard_levels(key, extent, cuts, least, high):
    def one(axis_at, parts):
        steps = jax.random.uniform(jax.random.fold_in(jax.random.fold_in(key, 6), axis_at), (parts,), jnp.float32, least / len(cuts), high / len(cuts))
        return jnp.repeat(jnp.exp(steps), extent[axis_at] // parts).reshape((-1,) + (1,) * (len(extent) - axis_at - 1))

    loudness = one(*cuts[0])
    for cut in cuts[1:]:
        loudness = loudness * one(*cut)
    return loudness


def noise(own_key, extent, spread, most, shards=(), held_as=jnp.bfloat16):
    factor_of = shard_levels(own_key, extent, shards, -0.22, 0.18) if shards else 1.0
    entries = jax.random.normal(own_key, extent, jnp.float32) * spread * factor_of
    return jnp.minimum(jnp.maximum(entries, -most), most).astype(held_as)


def setup_inputs(seed: int = 0) -> dict:
    arg_keys = jax.random.split(jax.random.key(seed), 10)
    queries = draw_queries(jax.random.fold_in(arg_keys[9], 71), 0)
    key_vectors = draw_key_vectors(jax.random.fold_in(arg_keys[9], 71), 0)
    value_vectors = noise(arg_keys[2], (TOKENS, D), 1.0, 6.0, ((0, 4), (1, 8)))
    step_sizes = jnp.clip(jnp.exp(math.log(0.003) - 2.3025851 * jax.random.uniform(arg_keys[3], (HEADS, TOKENS), jnp.float32) ** shard_levels(arg_keys[3], (HEADS, TOKENS), ((0, 8), (1, 4)), -0.2, 0.2)), 0.0003, 0.003)
    w_in = noise(arg_keys[4], (HEADS, HD, FH), HD ** -0.5, 0.25, ((0, 8),))
    w_up = noise(arg_keys[5], (HEADS, HD, FH), HD ** -0.5, 0.25, ((0, 8),))
    w_out = noise(arg_keys[6], (HEADS, HD, FH), (4 * FH) ** -0.5, 0.125, ((0, 8),))
    out_gate = noise(arg_keys[7], (TOKENS, D), 1.0, 6.0, ((0, 4), (1, 8)))
    norm_gain = jnp.clip(1.0 + 0.1 * jax.random.normal(arg_keys[8], (D,), jnp.float32), 0.5, 1.5)
    return {"queries": queries, "key_vectors": key_vectors, "value_vectors": value_vectors, "step_sizes": step_sizes, "w_in": w_in, "w_up": w_up, "w_out": w_out, "out_gate": out_gate, "norm_gain": norm_gain}


EPSILON = 1e-06

def silu_slope(pre):
    sigmoid = jax.nn.sigmoid(pre)
    return sigmoid * (1.0 + pre * (1.0 - sigmoid))

def block_attention(query_rows, key_rows, value_rows, first_query, first_key):
    scores = jnp.dot(query_rows, key_rows.T, preferred_element_type=jnp.float32) * query_rows.shape[1] ** (-0.5)
    query_pos = first_query + jnp.arange(query_rows.shape[0], dtype=jnp.int32)[:, None]
    key_pos = first_key + jnp.arange(key_rows.shape[0], dtype=jnp.int32)[None, :]
    distance = query_pos - key_pos
    allowed = (distance >= 0) & (distance < WINDOW) & (key_pos >= 0)
    masked = jnp.where(allowed, scores, -1e+30)
    largest = lax.optimization_barrier(jnp.max(masked, axis=1, keepdims=True))
    powered = jnp.where(allowed, jnp.exp(masked - largest), 0.0)
    weights = (powered / lax.optimization_barrier(jnp.sum(powered, axis=1, keepdims=True))).astype(jnp.bfloat16)
    return jnp.dot(weights, value_rows, preferred_element_type=jnp.float32)

def fast_increments(key_rows, value_rows, rate_rows, w_in, w_up, w_out):
    pre_gate = jnp.dot(key_rows, w_in, preferred_element_type=jnp.float32)
    pre_up = jnp.dot(key_rows, w_up, preferred_element_type=jnp.float32)
    hidden = (jax.nn.silu(pre_gate) * pre_up).astype(jnp.bfloat16)
    scaled = (rate_rows[:, None] * value_rows.astype(jnp.float32)).astype(jnp.bfloat16)
    backward = jnp.dot(scaled, w_out, preferred_element_type=jnp.float32)
    grad_gate = (backward * pre_up * silu_slope(pre_gate)).astype(jnp.bfloat16)
    grad_up = (backward * jax.nn.silu(pre_gate)).astype(jnp.bfloat16)
    return (jnp.dot(key_rows.T, grad_gate, preferred_element_type=jnp.float32), jnp.dot(key_rows.T, grad_up, preferred_element_type=jnp.float32), jnp.dot(scaled.T, hidden, preferred_element_type=jnp.float32))

def renormed(initial, increment):
    initial_f = initial.astype(jnp.float32)
    updated = initial_f + increment
    rescale = jnp.sqrt(lax.optimization_barrier(jnp.mean(initial_f * initial_f, axis=0)) + EPSILON) / jnp.sqrt(lax.optimization_barrier(jnp.mean(updated * updated, axis=0)) + EPSILON)
    return (updated * rescale).astype(jnp.bfloat16)

def apply_fast(query_rows, new_in, new_up, new_out):
    hidden = (jax.nn.silu(jnp.dot(query_rows, new_in, preferred_element_type=jnp.float32)) * jnp.dot(query_rows, new_up, preferred_element_type=jnp.float32)).astype(jnp.bfloat16)
    return lax.dot_general(hidden, new_out, (((1,), (1,)), ((), ())), preferred_element_type=jnp.float32)

def gated_norm(combined, out_gate, norm_gain):
    values_f = combined.astype(jnp.float32)
    mean_sq = lax.optimization_barrier(jnp.mean(values_f * values_f, axis=1, keepdims=True))
    return (values_f * lax.rsqrt(mean_sq + EPSILON) * norm_gain.astype(jnp.float32) * jax.nn.silu(out_gate.astype(jnp.float32))).astype(jnp.bfloat16)

def reference(queries, key_vectors, value_vectors, step_sizes, w_in, w_up, w_out, out_gate, norm_gain):
    head_count = w_in.shape[0]
    head_width = w_in.shape[1]

    def per_head(head_index):
        column_start = head_index * head_width
        q_head = lax.dynamic_slice_in_dim(queries, column_start, head_width, 1)
        k_head = lax.dynamic_slice_in_dim(key_vectors, column_start, head_width, 1)
        v_head = lax.dynamic_slice_in_dim(value_vectors, column_start, head_width, 1)
        rate_head = step_sizes[head_index]
        padded_keys = jnp.concatenate([jnp.zeros((WINDOW, head_width), k_head.dtype), k_head], axis=0)
        padded_values = jnp.concatenate([jnp.zeros((WINDOW, head_width), v_head.dtype), v_head], axis=0)

        def one_block(block_index):
            first = block_index * WINDOW
            q_rows = lax.dynamic_slice_in_dim(q_head, first, WINDOW, 0)
            k_rows = lax.dynamic_slice_in_dim(padded_keys, first, 2 * WINDOW, 0)
            v_rows = lax.dynamic_slice_in_dim(padded_values, first, 2 * WINDOW, 0)
            return block_attention(q_rows, k_rows, v_rows, first, first - WINDOW)
        attended = lax.map(one_block, jnp.arange(TOKENS // WINDOW, dtype=jnp.int32)).reshape(TOKENS, head_width)

        def one_shard(shard_index):
            first = shard_index * TOK_DEV
            partial_value = fast_increments(lax.dynamic_slice_in_dim(k_head, first, TOK_DEV, 0), lax.dynamic_slice_in_dim(v_head, first, TOK_DEV, 0), lax.dynamic_slice_in_dim(rate_head, first, TOK_DEV, 0), w_in[head_index], w_up[head_index], w_out[head_index])
            return (partial_value[0].astype(jnp.bfloat16), partial_value[1].astype(jnp.bfloat16), partial_value[2].astype(jnp.bfloat16))
        pieces = lax.map(one_shard, jnp.arange(N_CTX, dtype=jnp.int32))
        new_in = renormed(w_in[head_index], lax.optimization_barrier(jnp.sum(pieces[0].astype(jnp.float32), axis=0)))
        new_up = renormed(w_up[head_index], lax.optimization_barrier(jnp.sum(pieces[1].astype(jnp.float32), axis=0)))
        new_out = renormed(w_out[head_index], lax.optimization_barrier(jnp.sum(pieces[2].astype(jnp.float32), axis=0)))
        return (attended + apply_fast(q_head, new_in, new_up, new_out)).astype(jnp.bfloat16)
    heads_out = lax.map(per_head, jnp.arange(head_count, dtype=jnp.int32))
    combined = jnp.transpose(heads_out, (1, 0, 2)).reshape(TOKENS, head_count * head_width)
    return gated_norm(combined, out_gate, norm_gain)
```

```python
import functools
import math

import jax
import jax.numpy as jnp
from jax import lax
from jax.experimental import pallas as pl
from jax.experimental.pallas import tpu as pltpu
from jax.sharding import PartitionSpec as P

WINDOW = 1024
EPSILON = 1e-06
BQ = 256
PW = 128
F32 = jnp.float32
BF16 = jnp.bfloat16
NT = (((1,), (1,)), ((), ()))
TN = (((0,), (0,)), ((), ()))


def dotf(a, b, dims=None):
    if dims is None:
        return jnp.dot(a, b, preferred_element_type=F32)
    return lax.dot_general(a, b, dims, preferred_element_type=F32)


def as_column(row, width=128):
    return jnp.transpose(jnp.broadcast_to(row, (width, row.shape[1])))


def as_row(column):
    return jnp.transpose(jnp.broadcast_to(column, (column.shape[0], 128)))[:1]


def wide(x, width):
    return jnp.concatenate([x] * (width // x.shape[1]), axis=1)


def masked(scores, head_mask, tail_mask):
    row = lax.broadcasted_iota(jnp.int32, (BQ, BQ), 0)
    col = lax.broadcasted_iota(jnp.int32, (BQ, BQ), 1)
    width = scores.shape[1]
    parts = []
    low, high = 0, width
    if head_mask:
        parts.append(jnp.where(col > row, scores[:, :BQ], -1e30))
        low = BQ
    if tail_mask:
        high = width - BQ
    if high > low:
        parts.append(scores[:, low:high])
    if tail_mask:
        parts.append(jnp.where(col <= row, scores[:, high:], -1e30))
    return parts[0] if len(parts) == 1 else jnp.concatenate(parts, axis=1)


def attend(q, k, v, head_mask, tail_mask):
    scale = math.log2(math.e) * q.shape[1] ** (-0.5)
    s = masked(dotf(q, k, NT), head_mask, tail_mask)
    m = jnp.max(s, axis=1, keepdims=True)
    p = jnp.exp2((s - m) * scale)
    l = jnp.sum(p, axis=1, keepdims=True)
    return dotf(p.astype(BF16), v), m, l


def kernel(
    n_ctx, n_head, rows, hd, fh,
    q_hbm, k_hbm, v_hbm, step_ref, win_hbm, wup_hbm, wout_hbm, gate_hbm, gain_ref,
    out_hbm,
    q_ref, k_ref, v_ref, gate_ref, w_ref, new_ref,
    acc_ref, own_ref, rin_ref, lin_ref, rout_ref, lout_ref,
    att_ref, stat_ref, gq_ref, go_ref, gst_ref, oin_ref, ost_ref,
    z_ref, ss_ref, land_ref, sland_ref,
    load_sem, rsend, rrecv, lsend, lrecv, hsend, hrecv, asend, arecv, ssend, srecv, own_sem, out_sem,
):
    ci = lax.axis_index("ctx")
    hi = lax.axis_index("head")
    first, last = ci == 0, ci == n_ctx - 1
    not_first, not_last = ci > 0, ci < n_ctx - 1
    per = rows // n_head
    pieces = 3 * fh // PW
    width = fh // 2
    per_half = width // PW
    halo_blocks = WINDOW // BQ
    scale = math.log2(math.e) * hd ** (-0.5)

    loads = [
        pltpu.make_async_copy(win_hbm.at[0], w_ref.at[0], load_sem.at[0]),
        pltpu.make_async_copy(wup_hbm.at[0], w_ref.at[1], load_sem.at[1]),
        pltpu.make_async_copy(wout_hbm.at[0], w_ref.at[2], load_sem.at[2]),
        pltpu.make_async_copy(k_hbm, k_ref, load_sem.at[3]),
        pltpu.make_async_copy(v_hbm, v_ref, load_sem.at[4]),
        pltpu.make_async_copy(q_hbm, q_ref, load_sem.at[5]),
        pltpu.make_async_copy(gate_hbm, gate_ref, load_sem.at[6]),
    ]
    for load in loads:
        load.start()

    barrier = pltpu.get_barrier_semaphore()

    @pl.when(not_first)
    def _():
        pl.semaphore_signal(barrier, inc=1, device_id={"ctx": ci - 1})

    @pl.when(not_last)
    def _():
        pl.semaphore_signal(barrier, inc=1, device_id={"ctx": ci + 1})

    @pl.loop(1, n_head)
    def _(s):
        pl.semaphore_signal(barrier, inc=1, device_id={"head": lax.rem(hi + s, n_head)})

    pl.semaphore_wait(barrier, n_head - 1 + jnp.where(first, 0, 1) + jnp.where(last, 0, 1))

    def q_back():
        return pltpu.make_async_remote_copy(
            src_ref=q_hbm.at[pl.ds(0, WINDOW)], dst_ref=gq_ref, send_sem=hsend.at[0],
            recv_sem=hrecv.at[0], device_id={"ctx": ci - 1})

    def o_forward():
        return pltpu.make_async_remote_copy(
            src_ref=go_ref, dst_ref=oin_ref, send_sem=hsend.at[1],
            recv_sem=hrecv.at[1], device_id={"ctx": ci + 1})

    def st_forward():
        return pltpu.make_async_remote_copy(
            src_ref=gst_ref, dst_ref=ost_ref, send_sem=hsend.at[2],
            recv_sem=hrecv.at[2], device_id={"ctx": ci + 1})

    def to_right(p):
        return pltpu.make_async_remote_copy(
            src_ref=rout_ref.at[p], dst_ref=rin_ref.at[p], send_sem=rsend.at[p],
            recv_sem=rrecv.at[p], device_id={"ctx": ci + 1})

    def to_left(p):
        return pltpu.make_async_remote_copy(
            src_ref=lout_ref.at[p], dst_ref=lin_ref.at[p], send_sem=lsend.at[p],
            recv_sem=lrecv.at[p], device_id={"ctx": ci - 1})

    @pl.when(not_first)
    def _():
        q_back().start()

    for load in loads[:5]:
        load.wait()

    tb = rows // 4

    def increments(half):
        cols = pl.ds(half * width, width)
        acc_ref[...] = jnp.zeros_like(acc_ref)

        @pl.loop(0, rows // tb)
        def _(block):
            start = pl.multiple_of(block * tb, tb)
            span = pl.ds(start, tb)
            k = k_ref[span, :]
            rate = as_column(step_ref[:, span])
            scaled = (wide(rate, hd) * v_ref[span, :].astype(F32)).astype(BF16)
            gate = dotf(k, w_ref[0, :, cols])
            up = dotf(k, w_ref[1, :, cols])
            back = dotf(scaled, w_ref[2, :, cols])
            sig = jax.nn.sigmoid(gate)
            silu = gate * sig
            hidden = (silu * up).astype(BF16)
            g_gate = (back * up * (sig * (1.0 + gate * (1.0 - sig)))).astype(BF16)
            g_up = (back * silu).astype(BF16)
            acc_ref[:, : 2 * width] += dotf(k, jnp.concatenate([g_gate, g_up], axis=1), TN)
            acc_ref[:, 2 * width :] += dotf(scaled, hidden, TN)

        for x in range(3):
            for part in range(per_half):
                p = (half * 3 + x) * per_half + part
                base = x * width + part * PW
                piece = acc_ref[:, base : base + PW].astype(BF16)
                own_ref[p] = piece

                @pl.when(first)
                def _():
                    rout_ref[p] = piece
                    rin_ref[p] = jnp.zeros_like(piece)
                    to_right(p).start()

                @pl.when(last)
                def _():
                    lout_ref[p] = piece
                    lin_ref[p] = jnp.zeros_like(piece)
                    to_left(p).start()

    def chain(t):
        pr = t - (ci - 1)
        pleft = t - (n_ctx - 2 - ci)
        pd = t - (n_ctx - 2)

        @pl.when(not_first & (pr >= 0) & (pr < pieces))
        def _():
            to_right(pr).wait_recv()

            @pl.when(not_last)
            def _():
                rout_ref[pr] = (rin_ref[pr].astype(F32) + own_ref[pr].astype(F32)).astype(BF16)
                to_right(pr).start()

        @pl.when(not_last & (pleft >= 0) & (pleft < pieces))
        def _():
            to_left(pleft).wait_recv()

            @pl.when(not_first)
            def _():
                lout_ref[pleft] = (lin_ref[pleft].astype(F32) + own_ref[pleft].astype(F32)).astype(BF16)
                to_left(pleft).start()

        @pl.when((pd >= 0) & (pd < pieces))
        def _():
            x = lax.rem(pd // per_half, 3)
            col = (pd // (3 * per_half)) * width + lax.rem(pd, per_half) * PW
            cols = pl.ds(pl.multiple_of(col, PW), PW)
            before = w_ref[x, :, cols].astype(F32)
            total = own_ref[pd].astype(F32) + rin_ref[pd].astype(F32) + lin_ref[pd].astype(F32)
            after = before + total
            rescale = jnp.sqrt(jnp.mean(before * before, axis=0, keepdims=True) + EPSILON) / jnp.sqrt(
                jnp.mean(after * after, axis=0, keepdims=True) + EPSILON)
            new_ref[x, :, cols] = (after * rescale).astype(BF16)

    for half in range(2):
        increments(half)
    loads[5].wait()

    n_blocks = rows // BQ

    @pl.loop(halo_blocks, n_blocks)
    def _(b):
        start = pl.multiple_of(b * BQ, BQ)
        keys = pl.ds(pl.multiple_of(start - WINDOW, BQ), WINDOW + BQ)
        o, _, l = attend(q_ref[pl.ds(start, BQ), :], k_ref[keys, :], v_ref[keys, :], True, True)
        att_ref[pl.ds(start, BQ), :] = o / l
        chain(b - halo_blocks)

    t = n_blocks - halo_blocks
    for b in range(halo_blocks):
        span = pl.ds(b * BQ, BQ)
        keys = pl.ds(0, (b + 1) * BQ)
        o, m, l = attend(q_ref[span, :], k_ref[keys, :], v_ref[keys, :], False, True)
        att_ref[span, :] = o
        stat_ref[0, span, :] = jnp.broadcast_to(m, (BQ, 128))
        stat_ref[1, span, :] = jnp.broadcast_to(l, (BQ, 128))
        chain(t + b)
    t += halo_blocks

    @pl.when(not_last)
    def _():
        q_back().wait_recv()
        for b in range(halo_blocks):
            span = pl.ds(b * BQ, BQ)
            keys = pl.ds(rows - WINDOW + b * BQ, WINDOW - b * BQ)
            o, m, l = attend(gq_ref[span, :], k_ref[keys, :], v_ref[keys, :], True, False)
            go_ref[span, :] = o.astype(BF16)
            gst_ref[b] = jnp.concatenate([as_row(m), as_row(l), jnp.zeros((6, BQ), F32)], axis=0)
        o_forward().start()
        st_forward().start()

    @pl.loop(t, pieces + n_ctx - 2)
    def _(step):
        chain(step)

    loads[6].wait()

    @pl.when(first)
    def _():
        oin_ref[...] = jnp.zeros_like(oin_ref)
        ost_ref[...] = jnp.full_like(ost_ref, -1e30)

    gain = gain_ref[:, pl.ds(pl.multiple_of(hi * hd, hd), hd)]

    def rows_to(d):
        return pltpu.make_async_remote_copy(
            src_ref=z_ref.at[d], dst_ref=land_ref.at[hi], send_sem=asend.at[d],
            recv_sem=arecv.at[hi], device_id={"head": d})

    def squares_to(d):
        return pltpu.make_async_remote_copy(
            src_ref=ss_ref.at[d], dst_ref=sland_ref.at[hi], send_sem=ssend.at[d],
            recv_sem=srecv.at[hi], device_id={"head": d})

    def rows_from(s):
        return pltpu.make_async_remote_copy(
            src_ref=z_ref.at[s], dst_ref=land_ref.at[s], send_sem=asend.at[s],
            recv_sem=arecv.at[s], device_id={"head": s})

    def squares_from(s):
        return pltpu.make_async_remote_copy(
            src_ref=ss_ref.at[s], dst_ref=sland_ref.at[s], send_sem=ssend.at[s],
            recv_sem=srecv.at[s], device_id={"head": s})

    padded = ss_ref.shape[2]

    def apply(d):
        span = pl.ds(pl.multiple_of(d * per, 64), per)
        q = q_ref[span, :]
        gate = dotf(q, new_ref[0])
        up = dotf(q, new_ref[1])
        hidden = (jax.nn.silu(gate) * up).astype(BF16)
        combined = (att_ref[span, :] + dotf(hidden, new_ref[2], NT)).astype(BF16).astype(F32)
        og = gate_ref[span, :].astype(F32)
        z_ref[d] = (combined * gain * jax.nn.silu(og)).astype(BF16)
        square = (combined * combined).astype(BF16)
        if padded > per:
            square = jnp.concatenate([square, jnp.zeros((padded - per, hd), BF16)], axis=0)
        ss_ref[d] = dotf(jnp.ones((8, hd), BF16), square, NT)

        @pl.when(d != hi)
        def _():
            rows_to(d).start()
            squares_to(d).start()

    halo_chunks = -(-WINDOW // per)
    rest = n_head - halo_chunks

    @pl.loop(0, rest)
    def _(s):
        apply(halo_chunks + lax.rem(hi + s, rest))

    @pl.when(not_first)
    def _():
        o_forward().wait_recv()
        st_forward().wait_recv()

    for b in range(halo_blocks):
        span = pl.ds(b * BQ, BQ)
        m1, l1 = stat_ref[0, span, :], stat_ref[1, span, :]
        m2, l2 = as_column(ost_ref[b, :1]), as_column(ost_ref[b, 1:2])
        l2 = jnp.where(m2 > -1e29, l2, 0.0)
        m = jnp.maximum(m1, m2)
        e1 = jnp.exp2((m1 - m) * scale)
        e2 = jnp.exp2((m2 - m) * scale)
        inverse = 1.0 / (l1 * e1 + l2 * e2)
        att_ref[span, :] = att_ref[span, :] * wide(e1 * inverse, hd) + oin_ref[span, :].astype(F32) * wide(
            e2 * inverse, hd)

    @pl.loop(0, halo_chunks)
    def _(s):
        apply(lax.rem(hi + s, halo_chunks))

    own = pltpu.make_async_copy(z_ref.at[hi], land_ref.at[hi], own_sem.at[0])
    own.start()
    own_squares = pltpu.make_async_copy(ss_ref.at[hi], sland_ref.at[hi], own_sem.at[1])
    own_squares.start()
    own.wait()
    own_squares.wait()

    @pl.loop(1, n_head)
    def _(s):
        squares_from(lax.rem(hi + s, n_head)).wait_recv()

    total = sland_ref[0]
    for s in range(1, n_head):
        total = total + sland_ref[s]
    inv = lax.rsqrt(as_column(total[:1])[:per] * (1.0 / (n_head * hd)) + EPSILON)
    inv = wide(inv, hd)

    @pl.loop(1, n_head)
    def _(s):
        rows_from(lax.rem(hi + s, n_head)).wait_recv()

    @pl.loop(1, n_head)
    def _(s):
        d = lax.rem(hi + s, n_head)
        rows_to(d).wait_send()
        squares_to(d).wait_send()

    for s in range(n_head):
        z_ref[s] = (land_ref[s].astype(F32) * inv).astype(BF16)
        pltpu.make_async_copy(z_ref.at[s], out_hbm.at[:, pl.ds(s * hd, hd)], out_sem.at[s]).start()
    for s in range(n_head):
        pltpu.make_async_copy(z_ref.at[s], out_hbm.at[:, pl.ds(s * hd, hd)], out_sem.at[s]).wait()

    @pl.when(not_first)
    def _():
        q_back().wait_send()

        @pl.loop(0, pieces)
        def _(p):
            to_left(p).wait_send()

    @pl.when(not_last)
    def _():
        o_forward().wait_send()
        st_forward().wait_send()

        @pl.loop(0, pieces)
        def _(p):
            to_right(p).wait_send()


def per_device(q, k, v, steps, w_in, w_up, w_out, out_gate, norm_gain):
    n_ctx, n_head = lax.axis_size("ctx"), lax.axis_size("head")
    rows, hd = q.shape
    fh = w_in.shape[2]
    per = rows // n_head
    padded = -(-per // 128) * 128
    pieces = 3 * fh // PW
    halo_blocks = WINDOW // BQ
    any_spec = pl.BlockSpec(memory_space=pl.ANY)
    vmem = pl.BlockSpec(memory_space=pltpu.VMEM)
    V = pltpu.VMEM
    D = pltpu.SemaphoreType.DMA
    return pl.pallas_call(
        functools.partial(kernel, n_ctx, n_head, rows, hd, fh),
        out_shape=jax.ShapeDtypeStruct((per, n_head * hd), BF16),
        in_specs=[any_spec] * 3 + [vmem] + [any_spec] * 4 + [vmem],
        out_specs=any_spec,
        scratch_shapes=[
            V((rows, hd), BF16), V((rows, hd), BF16), V((rows, hd), BF16), V((rows, hd), BF16),
            V((3, hd, fh), BF16), V((3, hd, fh), BF16),
            V((hd, 3 * fh // 2), F32),
            V((pieces, hd, PW), BF16), V((pieces, hd, PW), BF16), V((pieces, hd, PW), BF16),
            V((pieces, hd, PW), BF16), V((pieces, hd, PW), BF16),
            V((rows, hd), F32), V((2, WINDOW, 128), F32),
            V((WINDOW, hd), BF16), V((WINDOW, hd), BF16), V((halo_blocks, 8, BQ), F32),
            V((WINDOW, hd), BF16), V((halo_blocks, 8, BQ), F32),
            V((n_head, per, hd), BF16), V((n_head, 8, padded), F32),
            V((n_head, per, hd), BF16), V((n_head, 8, padded), F32),
            D((7,)), D((pieces,)), D((pieces,)), D((pieces,)), D((pieces,)), D((3,)), D((3,)),
            D((n_head,)), D((n_head,)), D((n_head,)), D((n_head,)), D((2,)), D((n_head,)),
        ],
        compiler_params=pltpu.CompilerParams(
            collective_id=0, has_side_effects=True, vmem_limit_bytes=58 * 1024 * 1024),
    )(q, k, v, steps, w_in, w_up, w_out, out_gate, norm_gain.reshape(1, -1))


def solution(mesh):
    return jax.shard_map(
        per_device,
        mesh=mesh,
        in_specs=(
            P("ctx", "head"),
            P("ctx", "head"),
            P("ctx", "head"),
            P("head", "ctx"),
            P("head", None, None),
            P("head", None, None),
            P("head", None, None),
            P("ctx", "head"),
            P(),
        ),
        out_specs=P(("ctx", "head"), None),
        check_vma=False,
    )
```

```python
import functools
import math

import jax
import jax.numpy as jnp
from jax import lax
from jax.experimental import pallas as pl
from jax.experimental.pallas import tpu as pltpu
from jax.sharding import PartitionSpec as P

WINDOW = 1024
EPSILON = 1e-06
BQ = 256
PW = 128
F32 = jnp.float32
BF16 = jnp.bfloat16
NT = (((1,), (1,)), ((), ()))
TN = (((0,), (0,)), ((), ()))


def dotf(a, b, dims=None):
    if dims is None:
        return jnp.dot(a, b, preferred_element_type=F32)
    return lax.dot_general(a, b, dims, preferred_element_type=F32)


def as_column(row, width=128):
    return jnp.transpose(jnp.broadcast_to(row, (width, row.shape[1])))


def as_row(column):
    return jnp.transpose(jnp.broadcast_to(column, (column.shape[0], 128)))[:1]


def wide(x, width):
    return jnp.concatenate([x] * (width // x.shape[1]), axis=1)


def masked(scores, head_mask, tail_mask):
    row = lax.broadcasted_iota(jnp.int32, (BQ, BQ), 0)
    col = lax.broadcasted_iota(jnp.int32, (BQ, BQ), 1)
    width = scores.shape[1]
    parts = []
    low, high = 0, width
    if head_mask:
        parts.append(jnp.where(col > row, scores[:, :BQ], -1e30))
        low = BQ
    if tail_mask:
        high = width - BQ
    if high > low:
        parts.append(scores[:, low:high])
    if tail_mask:
        parts.append(jnp.where(col <= row, scores[:, high:], -1e30))
    return parts[0] if len(parts) == 1 else jnp.concatenate(parts, axis=1)


def attend(q, k, v, head_mask, tail_mask):
    scale = math.log2(math.e) * q.shape[1] ** (-0.5)
    s = masked(dotf(q, k, NT), head_mask, tail_mask)
    m = jnp.max(s, axis=1, keepdims=True)
    p = jnp.exp2((s - m) * scale)
    l = jnp.sum(p, axis=1, keepdims=True)
    return dotf(p.astype(BF16), v), m, l


def kernel(
    n_ctx, n_head, rows, hd, fh,
    q_hbm, k_hbm, v_hbm, step_ref, win_hbm, wup_hbm, wout_hbm, gate_hbm, gain_ref,
    out_hbm,
    q_ref, k_ref, v_ref, gate_ref, w_ref, new_ref,
    g_ref, h_ref, scaled_ref, acc_ref, own_ref, rin_ref, lin_ref, rout_ref, lout_ref,
    att_ref, stat_ref, gq_ref, go_ref, gst_ref, oin_ref, ost_ref,
    z_ref, ss_ref, land_ref, sland_ref,
    load_sem, rsend, rrecv, lsend, lrecv, hsend, hrecv, asend, arecv, ssend, srecv, own_sem, out_sem,
):
    ci = lax.axis_index("ctx")
    hi = lax.axis_index("head")
    first, last = ci == 0, ci == n_ctx - 1
    not_first, not_last = ci > 0, ci < n_ctx - 1
    per = rows // n_head
    pieces = 3 * fh // PW
    width = fh // 2
    per_half = width // PW
    halo_blocks = WINDOW // BQ
    scale = math.log2(math.e) * hd ** (-0.5)

    loads = [
        pltpu.make_async_copy(win_hbm.at[0], w_ref.at[0], load_sem.at[0]),
        pltpu.make_async_copy(wup_hbm.at[0], w_ref.at[1], load_sem.at[1]),
        pltpu.make_async_copy(wout_hbm.at[0], w_ref.at[2], load_sem.at[2]),
        pltpu.make_async_copy(k_hbm, k_ref, load_sem.at[3]),
        pltpu.make_async_copy(v_hbm, v_ref, load_sem.at[4]),
        pltpu.make_async_copy(q_hbm, q_ref, load_sem.at[5]),
        pltpu.make_async_copy(gate_hbm, gate_ref, load_sem.at[6]),
    ]
    for load in loads:
        load.start()

    barrier = pltpu.get_barrier_semaphore()

    @pl.when(not_first)
    def _():
        pl.semaphore_signal(barrier, inc=1, device_id={"ctx": ci - 1})

    @pl.when(not_last)
    def _():
        pl.semaphore_signal(barrier, inc=1, device_id={"ctx": ci + 1})

    @pl.loop(1, n_head)
    def _(s):
        pl.semaphore_signal(barrier, inc=1, device_id={"head": lax.rem(hi + s, n_head)})

    pl.semaphore_wait(barrier, n_head - 1 + jnp.where(first, 0, 1) + jnp.where(last, 0, 1))

    def q_back(b):
        span = pl.ds(b * BQ, BQ)
        return pltpu.make_async_remote_copy(
            src_ref=q_hbm.at[span], dst_ref=gq_ref.at[span], send_sem=hsend.at[b],
            recv_sem=hrecv.at[b], device_id={"ctx": ci - 1})

    def o_forward(b):
        span = pl.ds(b * BQ, BQ)
        sem = halo_blocks + b
        return pltpu.make_async_remote_copy(
            src_ref=go_ref.at[span], dst_ref=oin_ref.at[span], send_sem=hsend.at[sem],
            recv_sem=hrecv.at[sem], device_id={"ctx": ci + 1})

    def st_forward(b):
        sem = 2 * halo_blocks + b
        return pltpu.make_async_remote_copy(
            src_ref=gst_ref.at[b], dst_ref=ost_ref.at[b], send_sem=hsend.at[sem],
            recv_sem=hrecv.at[sem], device_id={"ctx": ci + 1})

    def to_right(p):
        return pltpu.make_async_remote_copy(
            src_ref=rout_ref.at[p], dst_ref=rin_ref.at[p], send_sem=rsend.at[p],
            recv_sem=rrecv.at[p], device_id={"ctx": ci + 1})

    def to_left(p):
        return pltpu.make_async_remote_copy(
            src_ref=lout_ref.at[p], dst_ref=lin_ref.at[p], send_sem=lsend.at[p],
            recv_sem=lrecv.at[p], device_id={"ctx": ci - 1})

    early = range(halo_blocks - 1, halo_blocks // 2 - 1, -1)
    late = range(halo_blocks // 2 - 1, -1, -1)

    @pl.when(not_first)
    def _():
        for b in early:
            q_back(b).start()

    for load in loads[:5]:
        load.wait()

    tb = rows // 4

    def increments(half, between):
        cols = pl.ds(half * width, width)

        @pl.loop(0, rows // tb)
        def _(block):
            start = pl.multiple_of(block * tb, tb)
            span = pl.ds(start, tb)
            k = k_ref[span, :]
            if half == 0:
                rate = as_column(step_ref[:, span])
                scaled_ref[span, :] = (wide(rate, hd) * v_ref[span, :].astype(F32)).astype(BF16)
            gate = dotf(k, w_ref[0, :, cols])
            up = dotf(k, w_ref[1, :, cols])
            back = dotf(scaled_ref[span, :], w_ref[2, :, cols])
            sig = jax.nn.sigmoid(gate)
            silu = gate * sig
            h_ref[span, :] = (silu * up).astype(BF16)
            g_ref[span, :width] = (back * up * (sig * (1.0 + gate * (1.0 - sig)))).astype(BF16)
            g_ref[span, width:] = (back * silu).astype(BF16)

        between(0)
        acc_ref[...] = jnp.zeros_like(acc_ref)

        @pl.loop(0, rows // tb)
        def _(block):
            span = pl.ds(pl.multiple_of(block * tb, tb), tb)
            acc_ref[:, : 2 * width] += dotf(k_ref[span, :], g_ref[span, :], TN)

        hand_on(half, (0, 1))
        between(1)

        @pl.loop(0, rows // tb)
        def _(block):
            span = pl.ds(pl.multiple_of(block * tb, tb), tb)
            acc_ref[:, 2 * width :] += dotf(scaled_ref[span, :], h_ref[span, :], TN)

        hand_on(half, (2,))
        between(2)

    def hand_on(half, which):
        for x in which:
            for part in range(per_half):
                p = (half * 3 + x) * per_half + part
                base = x * width + part * PW
                piece = acc_ref[:, base : base + PW].astype(BF16)
                own_ref[p] = piece

                @pl.when(first)
                def _():
                    rout_ref[p] = piece
                    rin_ref[p] = jnp.zeros_like(piece)
                    to_right(p).start()

                @pl.when(last)
                def _():
                    lout_ref[p] = piece
                    lin_ref[p] = jnp.zeros_like(piece)
                    to_left(p).start()

    def chain(t):
        pr = t - (ci - 1)
        pleft = t - (n_ctx - 2 - ci)
        pd = t - (n_ctx - 2)

        @pl.when(not_first & (pr >= 0) & (pr < pieces))
        def _():
            to_right(pr).wait_recv()

            @pl.when(not_last)
            def _():
                rout_ref[pr] = (rin_ref[pr].astype(F32) + own_ref[pr].astype(F32)).astype(BF16)
                to_right(pr).start()

        @pl.when(not_last & (pleft >= 0) & (pleft < pieces))
        def _():
            to_left(pleft).wait_recv()

            @pl.when(not_first)
            def _():
                lout_ref[pleft] = (lin_ref[pleft].astype(F32) + own_ref[pleft].astype(F32)).astype(BF16)
                to_left(pleft).start()

        @pl.when((pd >= 0) & (pd < pieces))
        def _():
            x = lax.rem(pd // per_half, 3)
            col = (pd // (3 * per_half)) * width + lax.rem(pd, per_half) * PW
            cols = pl.ds(pl.multiple_of(col, PW), PW)
            before = w_ref[x, :, cols].astype(F32)
            total = own_ref[pd].astype(F32) + rin_ref[pd].astype(F32) + lin_ref[pd].astype(F32)
            after = before + total
            rescale = jnp.sqrt(jnp.mean(before * before, axis=0, keepdims=True) + EPSILON) / jnp.sqrt(
                jnp.mean(after * after, axis=0, keepdims=True) + EPSILON)
            new_ref[x, :, cols] = (after * rescale).astype(BF16)

    increments(0, lambda step: None)
    increments(1, chain)

    @pl.when(not_first)
    def _():
        for b in late:
            q_back(b).start()

    loads[5].wait()

    n_blocks = rows // BQ

    @pl.loop(halo_blocks, n_blocks)
    def _(b):
        start = pl.multiple_of(b * BQ, BQ)
        keys = pl.ds(pl.multiple_of(start - WINDOW, BQ), WINDOW + BQ)
        o, _, l = attend(q_ref[pl.ds(start, BQ), :], k_ref[keys, :], v_ref[keys, :], True, True)
        att_ref[pl.ds(start, BQ), :] = o / l
        chain(b - halo_blocks + 3)

    t = n_blocks - halo_blocks + 3
    for b in range(halo_blocks):
        span = pl.ds(b * BQ, BQ)
        keys = pl.ds(0, (b + 1) * BQ)
        o, m, l = attend(q_ref[span, :], k_ref[keys, :], v_ref[keys, :], False, True)
        att_ref[span, :] = o
        stat_ref[0, span, :] = jnp.broadcast_to(m, (BQ, 128))
        stat_ref[1, span, :] = jnp.broadcast_to(l, (BQ, 128))
        chain(t + b)
    t += halo_blocks

    def guest(blocks):
        for b in blocks:
            q_back(b).wait_recv()
            span = pl.ds(b * BQ, BQ)
            keys = pl.ds(rows - WINDOW + b * BQ, WINDOW - b * BQ)
            o, m, l = attend(gq_ref[span, :], k_ref[keys, :], v_ref[keys, :], True, False)
            go_ref[span, :] = o.astype(BF16)
            gst_ref[b] = jnp.concatenate([as_row(m), as_row(l), jnp.zeros((6, BQ), F32)], axis=0)

    def forward(blocks):
        for b in blocks:
            o_forward(b).start()
            st_forward(b).start()

    @pl.when(not_last)
    def _():
        guest(early)

    @pl.loop(t, pieces + n_ctx - 2)
    def _(step):
        chain(step)

    @pl.when(not_last)
    def _():
        forward(early)

    loads[6].wait()

    @pl.when(first)
    def _():
        oin_ref[...] = jnp.zeros_like(oin_ref)
        ost_ref[...] = jnp.full_like(ost_ref, -1e30)

    gain = gain_ref[:, pl.ds(pl.multiple_of(hi * hd, hd), hd)]

    def rows_to(d):
        return pltpu.make_async_remote_copy(
            src_ref=z_ref.at[d], dst_ref=land_ref.at[hi], send_sem=asend.at[d],
            recv_sem=arecv.at[hi], device_id={"head": d})

    def squares_to(d):
        return pltpu.make_async_remote_copy(
            src_ref=ss_ref.at[d], dst_ref=sland_ref.at[hi], send_sem=ssend.at[d],
            recv_sem=srecv.at[hi], device_id={"head": d})

    def rows_from(s):
        return pltpu.make_async_remote_copy(
            src_ref=z_ref.at[s], dst_ref=land_ref.at[s], send_sem=asend.at[s],
            recv_sem=arecv.at[s], device_id={"head": s})

    def squares_from(s):
        return pltpu.make_async_remote_copy(
            src_ref=ss_ref.at[s], dst_ref=sland_ref.at[s], send_sem=ssend.at[s],
            recv_sem=srecv.at[s], device_id={"head": s})

    padded = ss_ref.shape[2]

    def apply(d):
        span = pl.ds(pl.multiple_of(d * per, 64), per)
        q = q_ref[span, :]
        gate = dotf(q, new_ref[0])
        up = dotf(q, new_ref[1])
        hidden = (jax.nn.silu(gate) * up).astype(BF16)
        combined = (att_ref[span, :] + dotf(hidden, new_ref[2], NT)).astype(BF16).astype(F32)
        og = gate_ref[span, :].astype(F32)
        z_ref[d] = (combined * gain * jax.nn.silu(og)).astype(BF16)
        square = (combined * combined).astype(BF16)
        if padded > per:
            square = jnp.concatenate([square, jnp.zeros((padded - per, hd), BF16)], axis=0)
        ss_ref[d] = dotf(jnp.ones((8, hd), BF16), square, NT)

        @pl.when(d != hi)
        def _():
            rows_to(d).start()
            squares_to(d).start()

    halo_chunks = -(-WINDOW // per)
    rest = n_head - halo_chunks

    @pl.loop(0, rest)
    def _(s):
        apply(halo_chunks + lax.rem(hi + s, rest))

    @pl.when(not_last)
    def _():
        for b in late:
            guest((b,))
            forward((b,))

    def combine(b):
        @pl.when(not_first)
        def _():
            o_forward(b).wait_recv()
            st_forward(b).wait_recv()

        span = pl.ds(b * BQ, BQ)
        m1, l1 = stat_ref[0, span, :], stat_ref[1, span, :]
        m2, l2 = as_column(ost_ref[b, :1]), as_column(ost_ref[b, 1:2])
        l2 = jnp.where(m2 > -1e29, l2, 0.0)
        m = jnp.maximum(m1, m2)
        e1 = jnp.exp2((m1 - m) * scale)
        e2 = jnp.exp2((m2 - m) * scale)
        inverse = 1.0 / (l1 * e1 + l2 * e2)
        att_ref[span, :] = att_ref[span, :] * wide(e1 * inverse, hd) + oin_ref[span, :].astype(F32) * wide(
            e2 * inverse, hd)

    done = halo_blocks
    for c in range(halo_chunks - 1, -1, -1):
        while done * BQ > c * per:
            done -= 1
            combine(done)
        apply(jnp.int32(c))

    own = pltpu.make_async_copy(z_ref.at[hi], land_ref.at[hi], own_sem.at[0])
    own.start()
    own_squares = pltpu.make_async_copy(ss_ref.at[hi], sland_ref.at[hi], own_sem.at[1])
    own_squares.start()
    own.wait()
    own_squares.wait()

    @pl.loop(1, n_head)
    def _(s):
        squares_from(lax.rem(hi + s, n_head)).wait_recv()

    total = sland_ref[0]
    for s in range(1, n_head):
        total = total + sland_ref[s]
    inv = lax.rsqrt(as_column(total[:1])[:per] * (1.0 / (n_head * hd)) + EPSILON)
    inv = wide(inv, hd)

    @pl.loop(1, n_head)
    def _(s):
        rows_from(lax.rem(hi + s, n_head)).wait_recv()

    @pl.loop(1, n_head)
    def _(s):
        d = lax.rem(hi + s, n_head)
        rows_to(d).wait_send()
        squares_to(d).wait_send()

    for s in range(n_head):
        z_ref[s] = (land_ref[s].astype(F32) * inv).astype(BF16)
        pltpu.make_async_copy(z_ref.at[s], out_hbm.at[:, pl.ds(s * hd, hd)], out_sem.at[s]).start()
    for s in range(n_head):
        pltpu.make_async_copy(z_ref.at[s], out_hbm.at[:, pl.ds(s * hd, hd)], out_sem.at[s]).wait()

    @pl.when(not_first)
    def _():
        for b in range(halo_blocks):
            q_back(b).wait_send()

        @pl.loop(0, pieces)
        def _(p):
            to_left(p).wait_send()

    @pl.when(not_last)
    def _():
        for b in range(halo_blocks):
            o_forward(b).wait_send()
            st_forward(b).wait_send()

        @pl.loop(0, pieces)
        def _(p):
            to_right(p).wait_send()


def per_device(q, k, v, steps, w_in, w_up, w_out, out_gate, norm_gain):
    n_ctx, n_head = lax.axis_size("ctx"), lax.axis_size("head")
    rows, hd = q.shape
    fh = w_in.shape[2]
    per = rows // n_head
    padded = -(-per // 128) * 128
    pieces = 3 * fh // PW
    halo_blocks = WINDOW // BQ
    any_spec = pl.BlockSpec(memory_space=pl.ANY)
    vmem = pl.BlockSpec(memory_space=pltpu.VMEM)
    V = pltpu.VMEM
    D = pltpu.SemaphoreType.DMA
    return pl.pallas_call(
        functools.partial(kernel, n_ctx, n_head, rows, hd, fh),
        out_shape=jax.ShapeDtypeStruct((per, n_head * hd), BF16),
        in_specs=[any_spec] * 3 + [vmem] + [any_spec] * 4 + [vmem],
        out_specs=any_spec,
        scratch_shapes=[
            V((rows, hd), BF16), V((rows, hd), BF16), V((rows, hd), BF16), V((rows, hd), BF16),
            V((3, hd, fh), BF16), V((3, hd, fh), BF16),
            V((rows, fh), BF16), V((rows, fh // 2), BF16), V((rows, hd), BF16), V((hd, 3 * fh // 2), F32),
            V((pieces, hd, PW), BF16), V((pieces, hd, PW), BF16), V((pieces, hd, PW), BF16),
            V((pieces, hd, PW), BF16), V((pieces, hd, PW), BF16),
            V((rows, hd), F32), V((2, WINDOW, 128), F32),
            V((WINDOW, hd), BF16), V((WINDOW, hd), BF16), V((halo_blocks, 8, BQ), F32),
            V((WINDOW, hd), BF16), V((halo_blocks, 8, BQ), F32),
            V((n_head, per, hd), BF16), V((n_head, 8, padded), F32),
            V((n_head, per, hd), BF16), V((n_head, 8, padded), F32),
            D((7,)), D((pieces,)), D((pieces,)), D((pieces,)), D((pieces,)), D((3 * halo_blocks,)), D((3 * halo_blocks,)),
            D((n_head,)), D((n_head,)), D((n_head,)), D((n_head,)), D((2,)), D((n_head,)),
        ],
        compiler_params=pltpu.CompilerParams(
            collective_id=0, has_side_effects=True, vmem_limit_bytes=58 * 1024 * 1024),
    )(q, k, v, steps, w_in, w_up, w_out, out_gate, norm_gain.reshape(1, -1))


def solution(mesh):
    return jax.shard_map(
        per_device,
        mesh=mesh,
        in_specs=(
            P("ctx", "head"),
            P("ctx", "head"),
            P("ctx", "head"),
            P("head", "ctx"),
            P("head", None, None),
            P("head", None, None),
            P("head", None, None),
            P("ctx", "head"),
            P(),
        ),
        out_specs=P(("ctx", "head"), None),
        check_vma=False,
    )
```
